32 devices in a mesh: fsdp: 8 (over z, x), seq: 4 (over y, core).
Axes of the slice: x: 2, y: 2, z: 4, core: 2. Of those that a mesh axis runs over, the one named last changes fastest.
Arguments:
- tokens: bfloat16 [8, 512, 768], P('fsdp', 'seq'), may hold values from -6 to 6
- encoder: bfloat16 [8, 512, 768], P('fsdp'), may hold values from -6 to 6
- dec_segments: int32 [8, 512], P('fsdp'), may hold values from 0 to 2, never falling along the last dimension, each value on 1 to 320 neighbouring positions
- enc_segments: int32 [8, 512], P('fsdp'), may hold values from 0 to 2, never falling along the last dimension, each value on 1 to 320 neighbouring positions
- buckets: int32 [512], replicated, may hold values from 0 to 31, as said below
- self_gain: bfloat16 [768], P(('fsdp', 'seq')), may hold values from 0.5 to 1.5
- self_query: bfloat16 [589824], P(('fsdp', 'seq')), may hold values from -0.0546875 to 0.0546875
- self_key: bfloat16 [589824], P(('fsdp', 'seq')), may hold values from -0.21875 to 0.21875
- self_value: bfloat16 [589824], P(('fsdp', 'seq')), may hold values from -0.21875 to 0.21875
- self_output: bfloat16 [589824], P(('fsdp', 'seq')), may hold values from -0.625 to 0.625
- bias_table: bfloat16 [32, 12], replicated, may hold values from -4 to 4
- cross_gain: bfloat16 [768], P(('fsdp', 'seq')), may hold values from 0.5 to 1.5
- cross_query: bfloat16 [589824], P(('fsdp', 'seq')), may hold values from -0.0546875 to 0.0546875
- cross_key: bfloat16 [589824], P(('fsdp', 'seq')), may hold values from -0.21875 to 0.21875
- cross_value: bfloat16 [589824], P(('fsdp', 'seq')), may hold values from -0.21875 to 0.21875
- cross_output: bfloat16 [589824], P(('fsdp', 'seq')), may hold values from -0.625 to 0.625
- ffn_gain: bfloat16 [768], P(('fsdp', 'seq')), may hold values from 0.5 to 1.5
- ffn_gate: bfloat16 [1572864], P(('fsdp', 'seq')), may hold values from -0.21875 to 0.21875
- ffn_up: bfloat16 [1572864], P(('fsdp', 'seq')), may hold values from -0.21875 to 0.21875
- ffn_down: bfloat16 [1572864], P(('fsdp', 'seq')), may hold values from -0.25 to 0.25
- cotangent: bfloat16 [8, 512, 768], P('fsdp', 'seq'), may hold values from -6 to 6
Outputs:
- output: bfloat16 [8, 512, 768], P('fsdp', 'seq')
- grad_tokens: float32 [8, 512, 768], P('fsdp', 'seq')
- grad_encoder: float32 [8, 512, 768], P('fsdp', 'seq')
- grad_self_gain: float32 [768], P(('fsdp', 'seq'))
- grad_self_query: float32 [589824], P(('fsdp', 'seq'))
- grad_self_key: float32 [589824], P(('fsdp', 'seq'))
- grad_self_value: float32 [589824], P(('fsdp', 'seq'))
- grad_self_output: float32 [589824], P(('fsdp', 'seq'))
- grad_bias_table: float32 [32, 12], replicated
- grad_cross_gain: float32 [768], P(('fsdp', 'seq'))
- grad_cross_query: float32 [589824], P(('fsdp', 'seq'))
- grad_cross_key: float32 [589824], P(('fsdp', 'seq'))
- grad_cross_value: float32 [589824], P(('fsdp', 'seq'))
- grad_cross_output: float32 [589824], P(('fsdp', 'seq'))
- grad_ffn_gain: float32 [768], P(('fsdp', 'seq'))
- grad_ffn_gate: float32 [1572864], P(('fsdp', 'seq'))
- grad_ffn_up: float32 [1572864], P(('fsdp', 'seq'))
- grad_ffn_down: float32 [1572864], P(('fsdp', 'seq'))
The draws below stay inside these ranges and needn't reach their ends.
Inputs may be any that keep to these rules, and one draw needn't show every extreme that they name: buckets[d] is the bucket of a key d positions before its query; it never falls as d grows, equals d for d below 16, and its last entry is 31. `dec_segments`: along each row the ids never fall; every id 0 to 2 appears; the longest document has 320 positions. `enc_segments`: along each row the ids never fall; every id 0 to 2 appears, so each decoder document has encoder positions in its row; the longest has 320 positions.
All inputs are finite; a program needn't handle non-finite values.
Results may differ from the reference program's by a relative error of at most 0.023.
The reference program's roundings to bfloat16 on the way count: a program that leaves them out, or rounds other values in their place, can miss the bound.
Values may be sent and summed in bfloat16 or wider, within the bound.
A program may use at most 256 MiB of HBM per device.

```python
import math
import jax
import jax.numpy as jnp
import numpy as np
from jax import lax

D = 768
HEADS = 12
HEAD_DIM = 64
FF = 2048
BUCKETS = 32
LEN = 512
ENC_LEN = 512
DOCS = 3
ROWS = 8
SEG_MOST = 320
ENC_MOST = 320


def draw_buckets(key, part):
    farther = jax.random.randint(key, (LEN - 16,), 16, BUCKETS)
    farther = jnp.sort(farther.astype(jnp.int32))
    farther = farther.at[LEN - 17].set(BUCKETS - 1)
    nearest = jnp.arange(16, dtype=jnp.int32)
    return jnp.concatenate([nearest, farther]).astype(jnp.int32)


def steps_of(key, dims, cuts, smallest, high):
    gain = 1.0
    for dim, shards_of in cuts:
        heights = jax.random.uniform(jax.random.fold_in(jax.random.fold_in(key, 6), dim), (shards_of,), jnp.float32, smallest / len(cuts), high / len(cuts))
        gain = gain * jnp.repeat(jnp.exp(heights), dims[dim] // shards_of).reshape((-1,) + (1,) * (len(dims) - 1 - dim))
    return gain


def profile(count, total, most, slope):
    weights = [(1 << 20) // math.isqrt(rank ** slope) + 1 for rank in range(2, count + 1)]
    surplus, given = total - most - (count - 1), [1] * (count - 1)
    while surplus > 0:
        movable = [i for i in range(count - 1) if given[i] < most]
        mass, left = sum([weights[i] for i in movable]), surplus
        for i in movable:
            more = min(most - given[i], max(1, left * weights[i] // mass), surplus)
            given[i] = given[i] + more
            surplus = surplus - more
    return np.array([most] + given)


def ragged(own_key, amount, total, limit, lean):
    if amount == 2:
        one = jax.random.randint(own_key, (), max(1, total - limit), min(limit, total - 1) + 1)
        return jnp.stack([one, total - one])
    lengths = jnp.asarray(profile(amount, total, limit, lean), jnp.int32)
    couples = (amount - 1) // 2
    giver, taker = lengths[1:1 + 2 * couples:2], lengths[2:2 + 2 * couples:2]
    slack = jnp.minimum(giver - 1, limit - taker)
    passed = jax.random.randint(jax.random.fold_in(own_key, 1), (couples,), 0, 1 << 20) % (slack + 1)
    lengths = lengths.at[1:1 + 2 * couples:2].set(giver - passed).at[2:2 + 2 * couples:2].set(taker + passed)
    return lengths[jax.random.permutation(jax.random.fold_in(own_key, 2), amount)]


def scatter_about(stream_key, extent, scale, reach, shards=(), kind=jnp.bfloat16):
    entries = jax.random.normal(stream_key, extent, jnp.float32) * scale
    if len(shards) > 0:
        entries = steps_of(stream_key, extent, shards, -0.22, 0.18) * entries
    return jnp.clip(entries, min=-reach, max=reach).astype(kind)


def setup_inputs(seed: int = 0) -> dict:
    splits = jax.random.split(jax.random.key(seed), 22)
    return {
        "tokens": scatter_about(splits[0], (ROWS, LEN, D), 1.0, 6.0, ((0, 8), (1, 4))),
        "encoder": scatter_about(splits[1], (ROWS, ENC_LEN, D), 1.0, 6.0, ((0, 8),)),
        "dec_segments": jax.vmap(lambda own: jnp.searchsorted(jnp.cumsum(ragged(own, DOCS, LEN, SEG_MOST, 1)), jnp.arange(LEN), side="right"))(jax.random.split(splits[2], ROWS)).reshape((ROWS, LEN)).astype(jnp.int32),
        "enc_segments": jax.vmap(lambda own: jnp.searchsorted(jnp.cumsum(ragged(own, DOCS, ENC_LEN, ENC_MOST, 1)), jnp.arange(ENC_LEN), side="right"))(jax.random.split(splits[3], ROWS)).reshape((ROWS, ENC_LEN)).astype(jnp.int32),
        "buckets": draw_buckets(jax.random.fold_in(splits[21], 71), 0),
        "self_gain": jnp.clip(1.0 + 0.1 * jax.random.normal(splits[5], (D,), jnp.float32), 0.5, 1.5).astype(jnp.bfloat16),
        "self_query": scatter_about(splits[6], (D * D,), (16 * D) ** -0.5, 0.0546875, ((0, 32),)),
        "self_key": scatter_about(splits[7], (D * D,), D ** -0.5, 0.21875, ((0, 32),)),
        "self_value": scatter_about(splits[8], (D * D,), D ** -0.5, 0.21875, ((0, 32),)),
        "self_output": scatter_about(splits[9], (D * D,), (D // 8) ** -0.5, 0.625, ((0, 32),)),
        "bias_table": scatter_about(splits[10], (BUCKETS, HEADS), 1.0, 4.0),
        "cross_gain": jnp.clip(1.0 + 0.1 * jax.random.normal(splits[11], (D,), jnp.float32), 0.5, 1.5).astype(jnp.bfloat16),
        "cross_query": scatter_about(splits[12], (D * D,), (16 * D) ** -0.5, 0.0546875, ((0, 32),)),
        "cross_key": scatter_about(splits[13], (D * D,), D ** -0.5, 0.21875, ((0, 32),)),
        "cross_value": scatter_about(splits[14], (D * D,), D ** -0.5, 0.21875, ((0, 32),)),
        "cross_output": scatter_about(splits[15], (D * D,), (D // 8) ** -0.5, 0.625, ((0, 32),)),
        "ffn_gain": jnp.clip(1.0 + 0.1 * jax.random.normal(splits[16], (D,), jnp.float32), 0.5, 1.5).astype(jnp.bfloat16),
        "ffn_gate": scatter_about(splits[17], (D * FF,), D ** -0.5, 0.21875, ((0, 32),)),
        "ffn_up": scatter_about(splits[18], (D * FF,), D ** -0.5, 0.21875, ((0, 32),)),
        "ffn_down": scatter_about(splits[19], (FF * D,), (FF // 4) ** -0.5, 0.25, ((0, 32),)),
        "cotangent": scatter_about(splits[20], (ROWS, LEN, D), 1.0, 6.0, ((0, 8), (1, 4))),
    }


@jax.custom_vjp
def low(v):
    return lax.optimization_barrier(v.astype(jnp.bfloat16)).astype(jnp.float32)

@jax.custom_vjp
def low_back(v):
    return v

def low_keep(v):
    return (low(v), None)

def low_pass(kept, grad):
    return (grad,)

def back_keep(v):
    return (v, None)

def back_low(kept, grad):
    return (low(grad),)
low.defvjp(low_keep, low_pass)
low_back.defvjp(back_keep, back_low)
epsilon = 1e-06
masked_value = -1e+30
highest = lax.Precision.HIGHEST

def rms_scale(values, gain_vector):
    factor = lax.rsqrt(lax.optimization_barrier(jnp.mean(values * values, axis=-1, keepdims=True)) + epsilon)
    return values * factor * gain_vector

def project(values, weight_matrix):
    return jnp.dot(values, weight_matrix, precision=highest)

def attention_row(query_row, key_row, value_row, position_bias, allowed):
    query_count = query_row.shape[0]
    key_count = key_row.shape[0]
    query_heads = query_row.reshape(query_count, HEADS, HEAD_DIM)
    key_heads = key_row.reshape(key_count, HEADS, HEAD_DIM)
    value_heads = value_row.reshape(key_count, HEADS, HEAD_DIM)
    scores = low_back(jnp.einsum('qhd,khd->hqk', query_heads, key_heads, precision=highest)) + position_bias
    scores = jnp.where(allowed[None], scores, masked_value)
    attn_probs = jax.nn.softmax(scores, axis=-1)
    mixed_heads = jnp.einsum('hqk,khd->qhd', low(attn_probs), value_heads, precision=highest)
    return mixed_heads.reshape(query_count, HEADS * HEAD_DIM)

def reference(tokens, encoder, dec_segments, enc_segments, buckets, self_gain, self_query, self_key, self_value, self_output, bias_table, cross_gain, cross_query, cross_key, cross_value, cross_output, ffn_gain, ffn_gate, ffn_up, ffn_down, cotangent):
    positions = jnp.arange(LEN, dtype=jnp.int32)
    distance = positions[:, None] - positions[None, :]
    bucket_index = buckets[jnp.clip(distance, 0, LEN - 1)]
    causal = distance >= 0
    self_allowed = causal[None] & (dec_segments[:, :, None] == dec_segments[:, None, :])
    cross_allowed = dec_segments[:, :, None] == enc_segments[:, None, :]

    def forward(inputs, enc_states, weights):
        gain_one, query_flat, key_flat, value_flat, output_flat, bias_weights, gain_two, query_flat_two, key_flat_two, value_flat_two, output_flat_two, gain_three, gate_flat, up_flat, down_flat = weights
        query_one = query_flat.reshape(D, D)
        key_one = key_flat.reshape(D, D)
        value_one = value_flat.reshape(D, D)
        output_one = output_flat.reshape(D, D)
        query_two = query_flat_two.reshape(D, D)
        key_two = key_flat_two.reshape(D, D)
        value_two = value_flat_two.reshape(D, D)
        output_two = output_flat_two.reshape(D, D)
        gate_weight = gate_flat.reshape(D, FF)
        up_weight = up_flat.reshape(D, FF)
        down_weight = down_flat.reshape(FF, D)
        inputs_flat = inputs.reshape(ROWS * LEN, D)
        norm_one = low(rms_scale(inputs_flat, gain_one))
        queries_one = low_back(low(project(norm_one, query_one))).reshape(ROWS, LEN, D)
        keys_one = low_back(low(project(norm_one, key_one))).reshape(ROWS, LEN, D)
        values_one = low_back(low(project(norm_one, value_one))).reshape(ROWS, LEN, D)
        position_bias = jnp.transpose(bias_weights[bucket_index], (2, 0, 1))

        def self_block(block_items):
            query_row, key_row, value_row, allowed = block_items
            return attention_row(query_row, key_row, value_row, position_bias, allowed)
        mixed_one = lax.map(jax.checkpoint(self_block), (queries_one, keys_one, values_one, self_allowed))
        mixed_one = low_back(low(mixed_one.reshape(ROWS * LEN, D)))
        hidden_one = inputs_flat + low_back(project(mixed_one, output_one))
        norm_two = low(rms_scale(hidden_one, gain_two))
        queries_two = low_back(low(project(norm_two, query_two))).reshape(ROWS, LEN, D)
        enc_flat = enc_states.reshape(ROWS * ENC_LEN, D)
        keys_two = low_back(low(project(enc_flat, key_two))).reshape(ROWS, ENC_LEN, D)
        values_two = low_back(low(project(enc_flat, value_two))).reshape(ROWS, ENC_LEN, D)

        def cross_block(block_items):
            query_row, key_row, value_row, allowed = block_items
            return attention_row(query_row, key_row, value_row, 0.0, allowed)
        mixed_two = lax.map(jax.checkpoint(cross_block), (queries_two, keys_two, values_two, cross_allowed))
        mixed_two = low_back(low(mixed_two.reshape(ROWS * LEN, D)))
        hidden_two = hidden_one + low_back(project(mixed_two, output_two))
        norm_three = low(rms_scale(hidden_two, gain_three))
        gate_value = low_back(project(norm_three, gate_weight))
        up_value = low_back(project(norm_three, up_weight))
        inner_act = low(jax.nn.gelu(gate_value, approximate=True) * up_value)
        result = hidden_two + low_back(project(inner_act, down_weight))
        return result.reshape(ROWS, LEN, D)
    weights = tuple((weight_item.astype(jnp.float32) for weight_item in (self_gain, self_query, self_key, self_value, self_output, bias_table, cross_gain, cross_query, cross_key, cross_value, cross_output, ffn_gain, ffn_gate, ffn_up, ffn_down)))
    result, pullback = jax.vjp(forward, tokens.astype(jnp.float32), encoder.astype(jnp.float32), weights)
    grad_inputs, grad_enc, grad_weights = pullback(cotangent.astype(jnp.float32))
    return (result.astype(jnp.bfloat16), grad_inputs, grad_enc, grad_weights[0], grad_weights[1], grad_weights[2], grad_weights[3], grad_weights[4], grad_weights[5], grad_weights[6], grad_weights[7], grad_weights[8], grad_weights[9], grad_weights[10], grad_weights[11], grad_weights[12], grad_weights[13], grad_weights[14])
```

```python
import jax
import jax.numpy as jnp
from jax import lax
from jax.sharding import PartitionSpec as P

HEADS = 12
HEAD_DIM = 64


epsilon = 1e-06
masked_value = -1e30
highest = lax.Precision.HIGHEST


def matmul(first_op, second_op):
    return jnp.dot(first_op, second_op, preferred_element_type=jnp.float32)


def contract_rows(first_op, second_op):
    return lax.dot_general(
        first_op, second_op, (((0,), (0,)), ((), ())), preferred_element_type=jnp.float32
    )


def times_transposed(first_op, second_op):
    return lax.dot_general(
        first_op, second_op, (((1,), (1,)), ((), ())), preferred_element_type=jnp.float32
    )


def rms_forward(values, gain_vector):
    factor = lax.rsqrt(jnp.mean(values * values, axis=-1, keepdims=True) + epsilon)
    return ((values * factor * gain_vector.astype(jnp.float32)).astype(jnp.bfloat16), factor)


def rms_backward(values, factor, gain_vector, upstream):
    scaled = upstream * gain_vector.astype(jnp.float32)
    inner_mean = jnp.mean(scaled * values, axis=-1, keepdims=True)
    grad_values = factor * scaled - values * (factor * factor * factor) * inner_mean
    grad_gain = jnp.sum(upstream * values * factor, axis=0)
    return (grad_values, grad_gain)


def gather_rows(packed):
    return lax.all_gather(packed, ("fsdp", "seq"), axis=0, tiled=True)


def scatter_rows(partial):
    return lax.psum_scatter(partial, ("fsdp", "seq"), scatter_dimension=0, tiled=True)


def scatter_to_owner(partial, row_count, block):
    count = lax.axis_size("seq")
    index = lax.axis_index("seq")
    total = lax.dynamic_slice_in_dim(partial, index * block, block, 1).astype(jnp.float32)
    for step in range(1, count):
        target = lax.rem(index + step, count)
        piece = lax.dynamic_slice_in_dim(partial, target * block, block, 1)
        pairs = [(source, (source + step) % count) for source in range(count)]
        total = total + lax.ppermute(piece, "seq", pairs).astype(jnp.float32)
    return total.astype(jnp.bfloat16)


def sum_everywhere(values):
    for axis in ("seq", "fsdp"):
        count = lax.axis_size(axis)
        step = 1
        while step < count:
            pairs = [(source, source ^ step) for source in range(count)]
            values = values + lax.ppermute(values, axis, pairs)
            step *= 2
    return values


def split_heads(values, row_count):
    return values.reshape(row_count, -1, HEADS, HEAD_DIM)


def score_block(query_heads, key_heads, position_bias, allowed):
    scores = (
        jnp.einsum("rqhd,rkhd->rhqk", query_heads, key_heads, preferred_element_type=jnp.float32)
        + position_bias
    )
    return jnp.where(allowed[:, None], scores, masked_value)


def attend(query_heads, key_heads, value_heads, position_bias, allowed):
    scores = score_block(query_heads, key_heads, position_bias, allowed)
    maximum = jnp.max(scores, axis=-1, keepdims=True)
    log_total = maximum + jnp.log(jnp.sum(jnp.exp(scores - maximum), axis=-1, keepdims=True))
    attn_probs = jnp.exp(scores - log_total).astype(jnp.bfloat16)
    mixed_heads = jnp.einsum(
        "rhqk,rkhd->rqhd", attn_probs, value_heads, preferred_element_type=jnp.float32
    )
    return (mixed_heads.astype(jnp.bfloat16), log_total)


def attend_back(query_heads, key_heads, value_heads, position_bias, allowed, log_total, grad_mixed):
    scores = score_block(query_heads, key_heads, position_bias, allowed)
    attn_probs = jnp.exp(scores - log_total)
    grad_probs = jnp.einsum(
        "rqhd,rkhd->rhqk", grad_mixed, value_heads, preferred_element_type=jnp.float32
    )
    grad_value = jnp.einsum(
        "rhqk,rqhd->rkhd",
        attn_probs.astype(jnp.bfloat16),
        grad_mixed,
        preferred_element_type=jnp.float32,
    )
    row_sums = jnp.sum(attn_probs * grad_probs, axis=-1, keepdims=True)
    grad_scores = attn_probs * (grad_probs - row_sums)
    low_scores = grad_scores.astype(jnp.bfloat16)
    grad_query = jnp.einsum(
        "rhqk,rkhd->rqhd", low_scores, key_heads, preferred_element_type=jnp.float32
    ).astype(jnp.bfloat16)
    grad_key = jnp.einsum(
        "rhqk,rqhd->rkhd", low_scores, query_heads, preferred_element_type=jnp.float32
    )
    return (grad_scores, grad_query, grad_key, grad_value)


def geglu(gate_part, up_part):
    return jax.nn.gelu(gate_part, approximate=True) * up_part


def per_device(
    tokens,
    encoder,
    dec_segments,
    enc_segments,
    buckets,
    self_gain,
    self_query,
    self_key,
    self_value,
    self_output,
    bias_table,
    cross_gain,
    cross_query,
    cross_key,
    cross_value,
    cross_output,
    ffn_gain,
    ffn_gate,
    ffn_up,
    ffn_down,
    cotangent,
):
    row_count, block_len, model_width = tokens.shape
    full_len = dec_segments.shape[1]
    enc_len = encoder.shape[1]
    seq_count = lax.axis_size("seq")
    seq_index = lax.axis_index("seq")
    enc_block = enc_len // seq_count
    inputs_flat = tokens.reshape(row_count * block_len, model_width).astype(jnp.float32)
    query_pos = seq_index * block_len + jnp.arange(block_len, dtype=jnp.int32)
    key_pos = jnp.arange(full_len, dtype=jnp.int32)
    distance = query_pos[:, None] - key_pos[None, :]
    bucket_ids = jnp.arange(bias_table.shape[0], dtype=jnp.int32)
    first = jnp.sum((buckets[None, :] < bucket_ids[:, None]).astype(jnp.int32), axis=1)
    beyond = jnp.sum((buckets[None, :] <= bucket_ids[:, None]).astype(jnp.int32), axis=1)
    clipped = jnp.clip(distance, 0, full_len - 1)[:, None, :]
    onehot = (
        (clipped >= first[None, :, None]) & (clipped < beyond[None, :, None])
    ).astype(jnp.bfloat16)
    position_bias = jnp.einsum(
        "qbk,bh->hqk", onehot, bias_table, preferred_element_type=jnp.float32
    )
    own_segments = lax.dynamic_slice_in_dim(dec_segments, seq_index * block_len, block_len, 1)
    self_allowed = (distance >= 0)[None] & (own_segments[:, :, None] == dec_segments[:, None, :])
    cross_allowed = own_segments[:, :, None] == enc_segments[:, None, :]
    own_rows = self_gain.shape[0]
    gains = jnp.pad(
        jnp.stack([self_gain, cross_gain, ffn_gain], axis=1), ((0, 0), (0, 125))
    )

    def rows_of(flat):
        return flat.reshape(own_rows, -1)

    packed_self = gather_rows(
        jnp.concatenate(
            [rows_of(w) for w in (self_query, self_key, self_value, self_output)] + [gains],
            axis=1,
        )
    )
    packed_rest = gather_rows(
        jnp.concatenate(
            [
                rows_of(w)
                for w in (
                    cross_query,
                    cross_key,
                    cross_value,
                    cross_output,
                    ffn_gate,
                    ffn_up,
                )
            ],
            axis=1,
        )
    )
    packed_cross = packed_rest[:, : 4 * model_width]
    packed_in = packed_rest[:, 4 * model_width :]
    packed_down = gather_rows(ffn_down.reshape(-1, model_width))
    all_gains = packed_self[:, 4 * model_width :]

    def columns(packed, index):
        return packed[:, index * model_width : (index + 1) * model_width]

    hidden_width = packed_down.shape[0]
    self_full = [all_gains[:, 0]] + [columns(packed_self, index) for index in range(4)]
    cross_full = [all_gains[:, 1]] + [columns(packed_cross, index) for index in range(4)]
    ffn_full = [
        all_gains[:, 2],
        packed_in[:, :hidden_width],
        packed_in[:, hidden_width:],
        packed_down,
    ]
    norm_one, factor_one = rms_forward(inputs_flat, self_full[0])
    qkv_one = matmul(norm_one, packed_self[:, : 3 * model_width]).astype(jnp.bfloat16)
    query_one = qkv_one[:, :model_width]
    pair_all = lax.all_gather(
        qkv_one[:, model_width:].reshape(row_count, block_len, 2 * model_width),
        "seq",
        axis=1,
        tiled=True,
    )
    key_all = pair_all[:, :, :model_width]
    value_all = pair_all[:, :, model_width:]
    query_heads_one = split_heads(query_one, row_count)
    key_heads_one = split_heads(key_all, row_count)
    value_heads_one = split_heads(value_all, row_count)
    mixed_one, lse_one = attend(
        query_heads_one, key_heads_one, value_heads_one, position_bias[None], self_allowed
    )
    mixed_one = mixed_one.reshape(row_count * block_len, model_width)
    hidden_one = inputs_flat + matmul(mixed_one, self_full[4])
    norm_two, factor_two = rms_forward(hidden_one, cross_full[0])
    query_two = matmul(norm_two, cross_full[1]).astype(jnp.bfloat16)
    enc_own = lax.dynamic_slice_in_dim(encoder, seq_index * enc_block, enc_block, 1).reshape(
        row_count * enc_block, model_width
    )
    enc_flat = encoder.reshape(row_count * enc_len, model_width)
    key_two = matmul(enc_flat, cross_full[2]).astype(jnp.bfloat16)
    value_two = matmul(enc_flat, cross_full[3]).astype(jnp.bfloat16)
    query_heads_two = split_heads(query_two, row_count)
    key_heads_two = split_heads(key_two, row_count)
    value_heads_two = split_heads(value_two, row_count)
    mixed_two, lse_two = attend(query_heads_two, key_heads_two, value_heads_two, 0.0, cross_allowed)
    mixed_two = mixed_two.reshape(row_count * block_len, model_width)
    hidden_two = hidden_one + matmul(mixed_two, cross_full[4])
    norm_three, factor_three = rms_forward(hidden_two, ffn_full[0])
    gate_value = matmul(norm_three, ffn_full[1])
    up_value = matmul(norm_three, ffn_full[2])
    activation, geglu_back = jax.vjp(geglu, gate_value, up_value)
    hidden_act = activation.astype(jnp.bfloat16)
    result = hidden_two + matmul(hidden_act, ffn_full[3])
    output = result.astype(jnp.bfloat16).reshape(row_count, block_len, model_width)
    self_back = self_full
    cross_back = cross_full
    ffn_back = ffn_full
    grad_out = cotangent.reshape(row_count * block_len, model_width).astype(jnp.float32)
    low_out = grad_out.astype(jnp.bfloat16)
    grad_down = contract_rows(hidden_act, low_out)
    grad_hidden = times_transposed(low_out, ffn_back[3])
    grad_gate, grad_up = geglu_back(grad_hidden)
    low_gate = grad_gate.astype(jnp.bfloat16)
    low_up = grad_up.astype(jnp.bfloat16)
    low_in = jnp.concatenate([low_gate, low_up], axis=1)
    summed_in = scatter_rows(contract_rows(norm_three, low_in).astype(jnp.bfloat16))
    summed_down = scatter_rows(grad_down.astype(jnp.bfloat16))
    grad_norm_three = times_transposed(low_in, packed_in)
    grad_residual_three, grad_gain_three = rms_backward(
        hidden_two, factor_three, ffn_back[0], grad_norm_three
    )
    grad_two = grad_out + grad_residual_three
    low_two = grad_two.astype(jnp.bfloat16)
    grad_cross_out = contract_rows(mixed_two, low_two)
    grad_mixed_two = times_transposed(low_two, cross_back[4]).astype(jnp.bfloat16)
    unused_scores, grad_query_two, grad_key_part_two, grad_value_part_two = attend_back(
        query_heads_two,
        key_heads_two,
        value_heads_two,
        0.0,
        cross_allowed,
        lse_two,
        split_heads(grad_mixed_two, row_count),
    )
    pair_two = jnp.concatenate(
        [
            grad_key_part_two.reshape(row_count, enc_len, model_width),
            grad_value_part_two.reshape(row_count, enc_len, model_width),
        ],
        axis=2,
    ).astype(jnp.bfloat16)
    low_pair_two = scatter_to_owner(pair_two, row_count, enc_block).reshape(
        row_count * enc_block, 2 * model_width
    )
    grad_cross_pair = contract_rows(enc_own, low_pair_two)
    grad_encoder = times_transposed(
        low_pair_two, packed_cross[:, model_width : 3 * model_width]
    ).reshape(row_count, enc_block, model_width)
    low_query_two = grad_query_two.reshape(row_count * block_len, model_width)
    grad_cross_query = contract_rows(norm_two, low_query_two)
    grad_norm_two = times_transposed(low_query_two, cross_back[1])
    summed_cross = scatter_rows(
        jnp.concatenate([grad_cross_query, grad_cross_pair, grad_cross_out], axis=1).astype(
            jnp.bfloat16
        )
    )
    grad_residual_two, grad_gain_two = rms_backward(
        hidden_one, factor_two, cross_back[0], grad_norm_two
    )
    grad_one = grad_two + grad_residual_two
    low_one = grad_one.astype(jnp.bfloat16)
    grad_self_out = contract_rows(mixed_one, low_one)
    grad_mixed_one = times_transposed(low_one, self_back[4]).astype(jnp.bfloat16)
    grad_scores_one, grad_query_one, grad_key_part_one, grad_value_part_one = attend_back(
        query_heads_one,
        key_heads_one,
        value_heads_one,
        position_bias[None],
        self_allowed,
        lse_one,
        split_heads(grad_mixed_one, row_count),
    )
    grad_table = jnp.einsum(
        "qbk,rhqk->bh", onehot.astype(jnp.float32), grad_scores_one, precision=highest
    )
    pair_one = jnp.concatenate(
        [
            grad_key_part_one.reshape(row_count, full_len, model_width),
            grad_value_part_one.reshape(row_count, full_len, model_width),
        ],
        axis=2,
    ).astype(jnp.bfloat16)
    low_pair_one = scatter_to_owner(pair_one, row_count, block_len).reshape(
        row_count * block_len, 2 * model_width
    )
    low_query_one = grad_query_one.reshape(row_count * block_len, model_width)
    low_qkv_one = jnp.concatenate([low_query_one, low_pair_one], axis=1)
    grad_self_qkv = contract_rows(norm_one, low_qkv_one)
    grad_norm_one = times_transposed(low_qkv_one, packed_self[:, : 3 * model_width])
    grad_residual_one, grad_gain_one = rms_backward(
        inputs_flat, factor_one, self_back[0], grad_norm_one
    )
    grad_tokens = (grad_one + grad_residual_one).reshape(row_count, block_len, model_width)
    summed_self = scatter_rows(
        jnp.concatenate([grad_self_qkv, grad_self_out], axis=1).astype(jnp.bfloat16)
    )
    table_items = grad_table.size
    small_parts = jnp.concatenate(
        [grad_table.reshape(-1), grad_gain_one, grad_gain_two, grad_gain_three]
    )
    small_sum = sum_everywhere(small_parts.reshape(-1, 128)).reshape(-1)
    table_grad = small_sum[:table_items].reshape(grad_table.shape)
    own_index = lax.axis_index("fsdp") * seq_count + seq_index

    def flat_columns(summed, start, width):
        return summed[:, start : start + width].reshape(-1).astype(jnp.float32)

    def gain_grad(index):
        start = table_items + index * model_width + own_index * own_rows
        return lax.dynamic_slice_in_dim(small_sum, start, own_rows, 0)

    return (
        output,
        grad_tokens,
        grad_encoder,
        gain_grad(0),
        *[flat_columns(summed_self, index * model_width, model_width) for index in range(4)],
        table_grad,
        gain_grad(1),
        *[flat_columns(summed_cross, index * model_width, model_width) for index in range(4)],
        gain_grad(2),
        flat_columns(summed_in, 0, hidden_width),
        flat_columns(summed_in, hidden_width, hidden_width),
        summed_down.reshape(-1).astype(jnp.float32),
    )


def solution(mesh):
    in_specs = (
        P("fsdp", "seq", None),
        P("fsdp", None, None),
        P("fsdp", None),
        P("fsdp", None),
        P(),
        P(("fsdp", "seq")),
        P(("fsdp", "seq")),
        P(("fsdp", "seq")),
        P(("fsdp", "seq")),
        P(("fsdp", "seq")),
        P(),
        P(("fsdp", "seq")),
        P(("fsdp", "seq")),
        P(("fsdp", "seq")),
        P(("fsdp", "seq")),
        P(("fsdp", "seq")),
        P(("fsdp", "seq")),
        P(("fsdp", "seq")),
        P(("fsdp", "seq")),
        P(("fsdp", "seq")),
        P("fsdp", "seq", None),
    )
    out_specs = (
        P("fsdp", "seq", None),
        P("fsdp", "seq", None),
        P("fsdp", "seq", None),
        P(("fsdp", "seq")),
        P(("fsdp", "seq")),
        P(("fsdp", "seq")),
        P(("fsdp", "seq")),
        P(("fsdp", "seq")),
        P(),
        P(("fsdp", "seq")),
        P(("fsdp", "seq")),
        P(("fsdp", "seq")),
        P(("fsdp", "seq")),
        P(("fsdp", "seq")),
        P(("fsdp", "seq")),
        P(("fsdp", "seq")),
        P(("fsdp", "seq")),
        P(("fsdp", "seq")),
    )
    return jax.shard_map(
        per_device, mesh=mesh, in_specs=in_specs, out_specs=out_specs, check_vma=False
    )
```

```python
import jax
import jax.numpy as jnp
from jax import lax
from jax.sharding import PartitionSpec as P

HEADS = 12
HEAD_DIM = 64


epsilon = 1e-06
masked_value = -1e30
highest = lax.Precision.HIGHEST


def matmul(first_op, second_op):
    return jnp.dot(first_op, second_op, preferred_element_type=jnp.float32)


def contract_rows(first_op, second_op):
    return lax.dot_general(
        first_op, second_op, (((0,), (0,)), ((), ())), preferred_element_type=jnp.float32
    )


def times_transposed(first_op, second_op):
    return lax.dot_general(
        first_op, second_op, (((1,), (1,)), ((), ())), preferred_element_type=jnp.float32
    )


def rms_forward(values, gain_vector):
    factor = lax.rsqrt(jnp.mean(values * values, axis=-1, keepdims=True) + epsilon)
    return ((values * factor * gain_vector.astype(jnp.float32)).astype(jnp.bfloat16), factor)


def rms_backward(values, factor, gain_vector, upstream):
    scaled = upstream * gain_vector.astype(jnp.float32)
    inner_mean = jnp.mean(scaled * values, axis=-1, keepdims=True)
    grad_values = factor * scaled - values * (factor * factor * factor) * inner_mean
    grad_gain = jnp.sum(upstream * values * factor, axis=0)
    return (grad_values, grad_gain)


def gather_rows(packed):
    return lax.all_gather(packed, ("fsdp", "seq"), axis=0, tiled=True)


def scatter_rows(partial):
    return lax.psum_scatter(partial, ("fsdp", "seq"), scatter_dimension=0, tiled=True)


def scatter_to_owner(partial, row_count, block):
    count = lax.axis_size("seq")
    index = lax.axis_index("seq")
    total = lax.dynamic_slice_in_dim(partial, index * block, block, 1).astype(jnp.float32)
    for step in range(1, count):
        target = lax.rem(index + step, count)
        piece = lax.dynamic_slice_in_dim(partial, target * block, block, 1)
        pairs = [(source, (source + step) % count) for source in range(count)]
        total = total + lax.ppermute(piece, "seq", pairs).astype(jnp.float32)
    return total.astype(jnp.bfloat16)


def gather_positions(own, full_len):
    count = lax.axis_size("seq")
    index = lax.axis_index("seq")
    block = own.shape[1]
    full = jnp.zeros((own.shape[0], full_len, own.shape[2]), own.dtype)
    full = lax.dynamic_update_slice_in_dim(full, own, index * block, 1)
    for step in range(1, count):
        pairs = [(source, (source + step) % count) for source in range(count)]
        origin = lax.rem(index + count - step, count)
        arrived = lax.ppermute(own, "seq", pairs)
        full = lax.dynamic_update_slice_in_dim(full, arrived, origin * block, 1)
    return full


def sum_everywhere(values):
    for axis in ("seq", "fsdp"):
        count = lax.axis_size(axis)
        step = 1
        while step < count:
            pairs = [(source, source ^ step) for source in range(count)]
            values = values + lax.ppermute(values, axis, pairs)
            step *= 2
    return values


def split_heads(values, row_count):
    return values.reshape(row_count, -1, HEADS, HEAD_DIM)


def score_block(query_heads, key_heads, position_bias, allowed):
    scores = (
        jnp.einsum("rqhd,rkhd->rhqk", query_heads, key_heads, preferred_element_type=jnp.float32)
        + position_bias
    )
    return jnp.where(allowed[:, None], scores, masked_value)


def attend(query_heads, key_heads, value_heads, position_bias, allowed):
    scores = score_block(query_heads, key_heads, position_bias, allowed)
    maximum = jnp.max(scores, axis=-1, keepdims=True)
    log_total = maximum + jnp.log(jnp.sum(jnp.exp(scores - maximum), axis=-1, keepdims=True))
    attn_probs = jnp.exp(scores - log_total).astype(jnp.bfloat16)
    mixed_heads = jnp.einsum(
        "rhqk,rkhd->rqhd", attn_probs, value_heads, preferred_element_type=jnp.float32
    )
    return (mixed_heads.astype(jnp.bfloat16), log_total)


def attend_back(query_heads, key_heads, value_heads, position_bias, allowed, log_total, grad_mixed):
    scores = score_block(query_heads, key_heads, position_bias, allowed)
    attn_probs = jnp.exp(scores - log_total)
    grad_probs = jnp.einsum(
        "rqhd,rkhd->rhqk", grad_mixed, value_heads, preferred_element_type=jnp.float32
    )
    grad_value = jnp.einsum(
        "rhqk,rqhd->rkhd",
        attn_probs.astype(jnp.bfloat16),
        grad_mixed,
        preferred_element_type=jnp.float32,
    )
    row_sums = jnp.sum(attn_probs * grad_probs, axis=-1, keepdims=True)
    grad_scores = attn_probs * (grad_probs - row_sums)
    low_scores = grad_scores.astype(jnp.bfloat16)
    grad_query = jnp.einsum(
        "rhqk,rkhd->rqhd", low_scores, key_heads, preferred_element_type=jnp.float32
    ).astype(jnp.bfloat16)
    grad_key = jnp.einsum(
        "rhqk,rqhd->rkhd", low_scores, query_heads, preferred_element_type=jnp.float32
    )
    return (grad_scores, grad_query, grad_key, grad_value)


def geglu(gate_part, up_part):
    return jax.nn.gelu(gate_part, approximate=True) * up_part


def per_device(
    tokens,
    encoder,
    dec_segments,
    enc_segments,
    buckets,
    self_gain,
    self_query,
    self_key,
    self_value,
    self_output,
    bias_table,
    cross_gain,
    cross_query,
    cross_key,
    cross_value,
    cross_output,
    ffn_gain,
    ffn_gate,
    ffn_up,
    ffn_down,
    cotangent,
):
    row_count, block_len, model_width = tokens.shape
    full_len = dec_segments.shape[1]
    enc_len = encoder.shape[1]
    seq_count = lax.axis_size("seq")
    seq_index = lax.axis_index("seq")
    enc_block = enc_len // seq_count
    inputs_flat = tokens.reshape(row_count * block_len, model_width).astype(jnp.float32)
    query_pos = seq_index * block_len + jnp.arange(block_len, dtype=jnp.int32)
    key_pos = jnp.arange(full_len, dtype=jnp.int32)
    distance = query_pos[:, None] - key_pos[None, :]
    bucket_ids = jnp.arange(bias_table.shape[0], dtype=jnp.int32)
    first = jnp.sum((buckets[None, :] < bucket_ids[:, None]).astype(jnp.int32), axis=1)
    beyond = jnp.sum((buckets[None, :] <= bucket_ids[:, None]).astype(jnp.int32), axis=1)
    clipped = jnp.clip(distance, 0, full_len - 1)[:, None, :]
    onehot = (
        (clipped >= first[None, :, None]) & (clipped < beyond[None, :, None])
    ).astype(jnp.bfloat16)
    position_bias = jnp.einsum(
        "qbk,bh->hqk", onehot, bias_table, preferred_element_type=jnp.float32
    )
    own_segments = lax.dynamic_slice_in_dim(dec_segments, seq_index * block_len, block_len, 1)
    self_allowed = (distance >= 0)[None] & (own_segments[:, :, None] == dec_segments[:, None, :])
    cross_allowed = own_segments[:, :, None] == enc_segments[:, None, :]
    own_rows = self_gain.shape[0]
    gains = jnp.pad(
        jnp.stack([self_gain, cross_gain, ffn_gain], axis=1), ((0, 0), (0, 125))
    )

    def rows_of(flat):
        return flat.reshape(own_rows, -1)

    packed_self = gather_rows(
        jnp.concatenate(
            [rows_of(w) for w in (self_query, self_key, self_value, self_output)] + [gains],
            axis=1,
        )
    )
    packed_rest = gather_rows(
        jnp.concatenate(
            [
                rows_of(w)
                for w in (
                    cross_query,
                    cross_key,
                    cross_value,
                    cross_output,
                    ffn_gate,
                    ffn_up,
                    ffn_down,
                )
            ],
            axis=1,
        )
    )
    packed_cross = packed_rest[:, : 4 * model_width]
    hidden_width = ffn_down.size // own_rows
    packed_in = packed_rest[:, 4 * model_width : 4 * model_width + 2 * hidden_width]
    packed_down = packed_rest[:, 4 * model_width + 2 * hidden_width :].reshape(
        hidden_width, model_width
    )
    all_gains = packed_self[:, 4 * model_width :]

    def columns(packed, index):
        return packed[:, index * model_width : (index + 1) * model_width]

    self_full = [all_gains[:, 0]] + [columns(packed_self, index) for index in range(4)]
    cross_full = [all_gains[:, 1]] + [columns(packed_cross, index) for index in range(4)]
    ffn_full = [
        all_gains[:, 2],
        packed_in[:, :hidden_width],
        packed_in[:, hidden_width:],
        packed_down,
    ]
    norm_one, factor_one = rms_forward(inputs_flat, self_full[0])
    qkv_one = matmul(norm_one, packed_self[:, : 3 * model_width]).astype(jnp.bfloat16)
    query_one = qkv_one[:, :model_width]
    pair_all = gather_positions(
        qkv_one[:, model_width:].reshape(row_count, block_len, 2 * model_width), full_len
    )
    key_all = pair_all[:, :, :model_width]
    value_all = pair_all[:, :, model_width:]
    query_heads_one = split_heads(query_one, row_count)
    key_heads_one = split_heads(key_all, row_count)
    value_heads_one = split_heads(value_all, row_count)
    mixed_one, lse_one = attend(
        query_heads_one, key_heads_one, value_heads_one, position_bias[None], self_allowed
    )
    mixed_one = mixed_one.reshape(row_count * block_len, model_width)
    hidden_one = inputs_flat + matmul(mixed_one, self_full[4])
    norm_two, factor_two = rms_forward(hidden_one, cross_full[0])
    query_two = matmul(norm_two, cross_full[1]).astype(jnp.bfloat16)
    enc_own = lax.dynamic_slice_in_dim(encoder, seq_index * enc_block, enc_block, 1).reshape(
        row_count * enc_block, model_width
    )
    enc_flat = encoder.reshape(row_count * enc_len, model_width)
    key_two = matmul(enc_flat, cross_full[2]).astype(jnp.bfloat16)
    value_two = matmul(enc_flat, cross_full[3]).astype(jnp.bfloat16)
    query_heads_two = split_heads(query_two, row_count)
    key_heads_two = split_heads(key_two, row_count)
    value_heads_two = split_heads(value_two, row_count)
    mixed_two, lse_two = attend(query_heads_two, key_heads_two, value_heads_two, 0.0, cross_allowed)
    mixed_two = mixed_two.reshape(row_count * block_len, model_width)
    hidden_two = hidden_one + matmul(mixed_two, cross_full[4])
    norm_three, factor_three = rms_forward(hidden_two, ffn_full[0])
    gate_value = matmul(norm_three, ffn_full[1])
    up_value = matmul(norm_three, ffn_full[2])
    activation, geglu_back = jax.vjp(geglu, gate_value, up_value)
    hidden_act = activation.astype(jnp.bfloat16)
    result = hidden_two + matmul(hidden_act, ffn_full[3])
    output = result.astype(jnp.bfloat16).reshape(row_count, block_len, model_width)
    self_back = self_full
    cross_back = cross_full
    ffn_back = ffn_full
    grad_out = cotangent.reshape(row_count * block_len, model_width).astype(jnp.float32)
    low_out = grad_out.astype(jnp.bfloat16)
    grad_down = contract_rows(hidden_act, low_out)
    grad_hidden = times_transposed(low_out, ffn_back[3])
    grad_gate, grad_up = geglu_back(grad_hidden)
    low_gate = grad_gate.astype(jnp.bfloat16)
    low_up = grad_up.astype(jnp.bfloat16)
    low_in = jnp.concatenate([low_gate, low_up], axis=1)
    summed_ffn = scatter_rows(
        jnp.concatenate(
            [
                contract_rows(norm_three, low_in).astype(jnp.bfloat16),
                grad_down.astype(jnp.bfloat16).reshape(model_width, hidden_width),
            ],
            axis=1,
        )
    )
    grad_norm_three = times_transposed(low_in, packed_in)
    grad_residual_three, grad_gain_three = rms_backward(
        hidden_two, factor_three, ffn_back[0], grad_norm_three
    )
    grad_two = grad_out + grad_residual_three
    low_two = grad_two.astype(jnp.bfloat16)
    grad_cross_out = contract_rows(mixed_two, low_two)
    grad_mixed_two = times_transposed(low_two, cross_back[4]).astype(jnp.bfloat16)
    unused_scores, grad_query_two, grad_key_part_two, grad_value_part_two = attend_back(
        query_heads_two,
        key_heads_two,
        value_heads_two,
        0.0,
        cross_allowed,
        lse_two,
        split_heads(grad_mixed_two, row_count),
    )
    pair_two = jnp.concatenate(
        [
            grad_key_part_two.reshape(row_count, enc_len, model_width),
            grad_value_part_two.reshape(row_count, enc_len, model_width),
        ],
        axis=2,
    ).astype(jnp.bfloat16)
    low_pair_two = scatter_to_owner(pair_two, row_count, enc_block).reshape(
        row_count * enc_block, 2 * model_width
    )
    grad_cross_pair = contract_rows(enc_own, low_pair_two)
    grad_encoder = times_transposed(
        low_pair_two, packed_cross[:, model_width : 3 * model_width]
    ).reshape(row_count, enc_block, model_width)
    low_query_two = grad_query_two.reshape(row_count * block_len, model_width)
    grad_cross_query = contract_rows(norm_two, low_query_two)
    grad_norm_two = times_transposed(low_query_two, cross_back[1])
    grad_residual_two, grad_gain_two = rms_backward(
        hidden_one, factor_two, cross_back[0], grad_norm_two
    )
    grad_one = grad_two + grad_residual_two
    low_one = grad_one.astype(jnp.bfloat16)
    grad_self_out = contract_rows(mixed_one, low_one)
    grad_mixed_one = times_transposed(low_one, self_back[4]).astype(jnp.bfloat16)
    grad_scores_one, grad_query_one, grad_key_part_one, grad_value_part_one = attend_back(
        query_heads_one,
        key_heads_one,
        value_heads_one,
        position_bias[None],
        self_allowed,
        lse_one,
        split_heads(grad_mixed_one, row_count),
    )
    grad_table = jnp.einsum(
        "qbk,rhqk->bh", onehot.astype(jnp.float32), grad_scores_one, precision=highest
    )
    pair_one = jnp.concatenate(
        [
            grad_key_part_one.reshape(row_count, full_len, model_width),
            grad_value_part_one.reshape(row_count, full_len, model_width),
        ],
        axis=2,
    ).astype(jnp.bfloat16)
    low_pair_one = scatter_to_owner(pair_one, row_count, block_len).reshape(
        row_count * block_len, 2 * model_width
    )
    low_query_one = grad_query_one.reshape(row_count * block_len, model_width)
    low_qkv_one = jnp.concatenate([low_query_one, low_pair_one], axis=1)
    grad_self_qkv = contract_rows(norm_one, low_qkv_one)
    grad_norm_one = times_transposed(low_qkv_one, packed_self[:, : 3 * model_width])
    grad_residual_one, grad_gain_one = rms_backward(
        inputs_flat, factor_one, self_back[0], grad_norm_one
    )
    grad_tokens = (grad_one + grad_residual_one).reshape(row_count, block_len, model_width)
    summed_attention = scatter_rows(
        jnp.concatenate(
            [grad_self_qkv, grad_self_out, grad_cross_query, grad_cross_pair, grad_cross_out],
            axis=1,
        ).astype(jnp.bfloat16)
    )
    table_items = grad_table.size
    small_parts = jnp.concatenate(
        [grad_table.reshape(-1), grad_gain_one, grad_gain_two, grad_gain_three]
    )
    small_sum = sum_everywhere(small_parts.reshape(-1, 128)).reshape(-1)
    table_grad = small_sum[:table_items].reshape(grad_table.shape)
    own_index = lax.axis_index("fsdp") * seq_count + seq_index

    def flat_columns(summed, start, width):
        return summed[:, start : start + width].reshape(-1).astype(jnp.float32)

    def gain_grad(index):
        start = table_items + index * model_width + own_index * own_rows
        return lax.dynamic_slice_in_dim(small_sum, start, own_rows, 0)

    return (
        output,
        grad_tokens,
        grad_encoder,
        gain_grad(0),
        *[flat_columns(summed_attention, index * model_width, model_width) for index in range(4)],
        table_grad,
        gain_grad(1),
        *[flat_columns(summed_attention, index * model_width, model_width) for index in range(4, 8)],
        gain_grad(2),
        *[flat_columns(summed_ffn, index * hidden_width, hidden_width) for index in range(3)],
    )


def solution(mesh):
    in_specs = (
        P("fsdp", "seq", None),
        P("fsdp", None, None),
        P("fsdp", None),
        P("fsdp", None),
        P(),
        P(("fsdp", "seq")),
        P(("fsdp", "seq")),
        P(("fsdp", "seq")),
        P(("fsdp", "seq")),
        P(("fsdp", "seq")),
        P(),
        P(("fsdp", "seq")),
        P(("fsdp", "seq")),
        P(("fsdp", "seq")),
        P(("fsdp", "seq")),
        P(("fsdp", "seq")),
        P(("fsdp", "seq")),
        P(("fsdp", "seq")),
        P(("fsdp", "seq")),
        P(("fsdp", "seq")),
        P("fsdp", "seq", None),
    )
    out_specs = (
        P("fsdp", "seq", None),
        P("fsdp", "seq", None),
        P("fsdp", "seq", None),
        P(("fsdp", "seq")),
        P(("fsdp", "seq")),
        P(("fsdp", "seq")),
        P(("fsdp", "seq")),
        P(("fsdp", "seq")),
        P(),
        P(("fsdp", "seq")),
        P(("fsdp", "seq")),
        P(("fsdp", "seq")),
        P(("fsdp", "seq")),
        P(("fsdp", "seq")),
        P(("fsdp", "seq")),
        P(("fsdp", "seq")),
        P(("fsdp", "seq")),
        P(("fsdp", "seq")),
    )
    return jax.shard_map(
        per_device, mesh=mesh, in_specs=in_specs, out_specs=out_specs, check_vma=False
    )
```
